512 devices in a mesh: span: 16 (over x, z_hi, core), seq: 32 (over y, z_lo).
Axes of the slice: x: 4, y: 4, z: 16 (z_hi: 2, z_lo: 8; z = z_hi * 8 + z_lo), core: 2. Of those that a mesh axis runs over, the one named last changes fastest.
Arguments:
- queries: bfloat16 [16, 1024, 4096], P('span', 'seq')
- keys: bfloat16 [16, 1024, 4096], P('span', 'seq')
- values: bfloat16 [16, 1024, 4096], P('span', 'seq'), may hold values from -6 to 6
- lengths: int32 [16], replicated, may hold values from 256 to 1024, as said below
- span_mask: int32 [16, 2], replicated, may hold values from 0 to 1, as said below
- levels: int32 [16], replicated, may hold values from 0 to 15, each once
- level_gain: float32 [16, 4096], replicated, may hold values from 0.1 to 1.9
Outputs:
- attended: bfloat16 [16, 1024, 4096], P('span', 'seq')
The draws below stay inside these ranges and needn't reach their ends.
Inputs may be any that keep to these rules, and one draw needn't show every extreme that they name: `lengths`: each span has at least 256 live tokens; some span has all 1024. `span_mask`: entries with c - 1 - j < 0 are 0.
All inputs are finite; a program needn't handle non-finite values.
Results may differ from the reference program's by a relative error of at most 0.0047.
Values may be sent and summed in bfloat16 or wider, within the bound.
A program may use at most 64 MiB of HBM per device.

```python
import jax
import jax.numpy as jnp
from jax import lax

HEADS = 32
HD = 128
WIN = 2
CTOK = 1024
SPANS = 16
F = 4096


def draw_queries(key, part):
    key = jax.random.fold_in(key, 1)
    result = jnp.clip(jax.random.normal(key, (SPANS, CTOK, F), jnp.float32), -6.0, 6.0)
    return result.astype(jnp.bfloat16)


def draw_keys(key, part):
    key = jax.random.fold_in(key, 2)
    result = jnp.clip(jax.random.normal(key, (SPANS, CTOK, F), jnp.float32), -6.0, 6.0)
    return result.astype(jnp.bfloat16)


def draw_lengths(key, part):
    key = jax.random.fold_in(key, 3)
    first, second = jax.random.split(key)
    counts = jax.random.randint(first, (SPANS,), CTOK // 4, CTOK + 1)
    fullest = jax.random.randint(second, (), 0, SPANS)
    return jnp.where(jnp.arange(SPANS) == fullest, CTOK, counts).astype(jnp.int32)


def draw_span_mask(key, part):
    key = jax.random.fold_in(key, 4)
    coins = jax.random.randint(key, (SPANS, WIN), 0, 4)
    rows = jnp.arange(SPANS)[:, None]
    steps = jnp.arange(WIN)[None, :]
    return jnp.where((coins > 0) & (rows - 1 - steps >= 0), 1, 0).astype(jnp.int32)


def block_levels(stream_key, shape, cuts, smallest, high):
    level = 1.0
    for position, blocks in cuts:
        steps = jax.random.uniform(jax.random.fold_in(jax.random.fold_in(stream_key, 6), position), (blocks,), jnp.float32, smallest / len(cuts), high / len(cuts))
        level = level * jnp.repeat(jnp.exp(steps), shape[position] // blocks).reshape((-1,) + (1,) * (len(shape) - 1 - position))
    return level


def normal_values(stream_key, extent, deviation, most, cuts=(), held_as=jnp.bfloat16):
    values = deviation * jax.random.normal(stream_key, extent, jnp.float32)
    if cuts:
        values = values * block_levels(stream_key, extent, cuts, -0.22, 0.18)
    return jnp.clip(values, -most, most).astype(held_as)


def setup_inputs(seed: int = 0) -> dict:
    key_list = jax.random.split(jax.random.key(seed), 8)
    return {
        "queries": draw_queries(jax.random.fold_in(key_list[7], 71), 0),
        "keys": draw_keys(jax.random.fold_in(key_list[7], 71), 0),
        "values": normal_values(key_list[2], (SPANS, CTOK, F), 1.0, 6.0, ((0, 16), (1, 32))),
        "lengths": draw_lengths(jax.random.fold_in(key_list[7], 71), 0),
        "span_mask": draw_span_mask(jax.random.fold_in(key_list[7], 71), 0),
        "levels": jax.random.permutation(key_list[5], SPANS).astype(jnp.int32),
        "level_gain": jnp.clip(1.0 + 0.18 * jax.random.normal(key_list[6], (SPANS, F), jnp.float32), 0.1, 1.9),
    }


def reference(queries, keys, values, lengths, span_mask, levels, level_gain):
    scale = 1.0 / jnp.sqrt(jnp.float32(HD))
    slots = jnp.arange(CTOK, dtype=jnp.int32)

    def one_span(index):
        query_block = lax.dynamic_index_in_dim(queries, index, 0, False).reshape(CTOK, HEADS, HD)
        key_parts = []
        value_parts = []
        valid_parts = []
        for step in range(WIN + 1):
            source = jnp.maximum(index - step, 0).astype(jnp.int32)
            key_parts.append(lax.dynamic_index_in_dim(keys, source, 0, False).reshape(CTOK, HEADS, HD))
            value_parts.append(lax.dynamic_index_in_dim(values, source, 0, False).reshape(CTOK, HEADS, HD))
            live = slots < lengths[source]
            if step > 0:
                live = live & (index - step >= 0) & (span_mask[index, step - 1] == 1)
            valid_parts.append(live)
        key_all = jnp.concatenate(key_parts, 0)
        value_all = jnp.concatenate(value_parts, 0)
        valid = jnp.concatenate(valid_parts, 0)
        scores = jnp.einsum('qhd,khd->hqk', query_block.astype(jnp.float32), key_all.astype(jnp.float32)) * scale
        scores = jnp.where(valid[None, None, :], scores, jnp.float32(-1e+30))
        top = lax.optimization_barrier(jnp.max(scores, axis=-1, keepdims=True))
        expd = jnp.where(valid[None, None, :], jnp.exp(scores - top), jnp.float32(0.0))
        total = lax.optimization_barrier(jnp.sum(expd, axis=-1))
        probs = expd.astype(jnp.bfloat16)
        summed = jnp.einsum('hqk,khd->qhd', probs.astype(jnp.float32), value_all.astype(jnp.float32))
        mixed = summed / jnp.transpose(total)[:, :, None]
        gain_row = level_gain[levels[index]].reshape(HEADS, HD)
        return (mixed * gain_row[None, :, :]).astype(jnp.bfloat16).reshape(CTOK, F)
    return lax.map(one_span, jnp.arange(SPANS, dtype=jnp.int32))
```

```python
import functools

import jax
import jax.numpy as jnp
from jax import lax
from jax.experimental import pallas as pl
from jax.experimental.pallas import tpu as pltpu
from jax.sharding import PartitionSpec as P

HD = 128
WIN = 2
NX, NY, NZ = 4, 4, 8
CORES = 2
QB = 128
MESH = pl.DeviceIdType.MESH
NEG = -1e30
LOG2E = 1.4426950408889634


def low_bit(pair):
    return 1 - lax.rem(pair + 2, 8) // 4


def attend_kernel(
    lengths, span_mask, levels, q_in, k_in, v_in, gain_in, out,
    q_buf, k_buf, v_buf, o_buf, gain_buf,
    send_k, send_v, send_q, send_o, send_shift,
    recv_k, recv_v, recv_q, recv_o, gain_sem,
):
    rows = q_in.shape[0]
    slots = k_buf.shape[1]
    span_count = lengths.shape[0]
    chunk = slots // NY
    here = lax.axis_index("span")
    member = lax.axis_index("seq")
    x, z_hi, core = here // 4, lax.rem(here // 2, 2), lax.rem(here, 2)
    y, z_lo = member // NZ, lax.rem(member, NZ)
    z = z_hi * NZ + z_lo
    pair, bit = z // 2, lax.rem(z, 2)
    upper = (bit + low_bit(pair)) - 2 * bit * low_bit(pair)
    span = 4 * x + 2 * upper + core
    head = y * NZ + pair
    stays = upper == z_hi

    def device(xx, yy, zz, cc):
        return (xx * 4 + (zz // NZ) * 2 + cc, yy * NZ + lax.rem(zz, NZ))

    def head_place(pp):
        first = low_bit(pp)
        return 2 * pp + first + z_hi * (1 - 2 * first)

    flipped = z + 1 - 2 * bit
    next_x = lax.rem(x + upper, NX)
    prev_x = lax.rem(x + NX - 1 + upper, NX)

    barrier = pltpu.get_barrier_semaphore()

    def greet(index, carry):
        yy, zz = index // NZ, lax.rem(index, NZ)

        @pl.when(jnp.logical_not(stays & (index == member)))
        def _():
            pl.semaphore_signal(
                barrier, inc=1, device_id=device(x, yy, upper * NZ + zz, core), device_id_type=MESH
            )

        return carry

    lax.fori_loop(0, NY * NZ, greet, 0)

    @pl.when(core == 0)
    def _():
        for cc in range(CORES):
            pl.semaphore_signal(
                barrier, inc=1, device_id=device(prev_x, y, flipped, cc), device_id_type=MESH
            )

    @pl.when(core == 1)
    def _():
        pl.semaphore_signal(barrier, inc=1, device_id=device(x, y, z, 0), device_id_type=MESH)

    gain_copy = pltpu.make_async_copy(
        gain_in.at[:, pl.ds(pl.multiple_of(head * HD, HD), HD)], gain_buf, gain_sem
    )
    gain_copy.start()

    pl.semaphore_wait(barrier, NY * NZ + 2 - core - jnp.where(stays, 1, 0))

    def exchange(source, landing, send_sem, recv_sem):
        def step(index, carry):
            turn, place = index // NZ, NZ - 1 - lax.rem(index, NZ)
            yy = lax.rem(y + turn, NY)
            away = ((place + 1) // 2) * (2 * lax.rem(place, 2) - 1)
            pp = lax.rem(pair + away + NZ, NZ)
            zz = head_place(pp)
            columns = pl.ds(pl.multiple_of((yy * NZ + pp) * HD, HD), HD)
            block = source.at[:, columns]
            target = landing.at[pl.ds(pl.multiple_of(member * rows, rows), rows), :]
            own = (yy == y) & (zz == z)

            @pl.when(own)
            def _():
                pltpu.make_async_copy(block, target, recv_sem).start()

            @pl.when(jnp.logical_not(own))
            def _():
                pltpu.make_async_remote_copy(
                    src_ref=block, dst_ref=target, send_sem=send_sem, recv_sem=recv_sem,
                    device_id=device(x, yy, zz, core), device_id_type=MESH,
                ).start()

            return carry

        lax.fori_loop(0, NY * NZ, step, 0)

    exchange(k_in, k_buf.at[0], send_k, recv_k.at[0])
    exchange(v_in, v_buf.at[0], send_v, recv_v.at[0])
    exchange(q_in, q_buf, send_q, recv_q.at[y])

    def landed(ref, sem):
        pltpu.make_async_copy(ref, ref, sem).wait()

    def shift(buf, from_slot, to_slot, send_sem, recv, target):
        return pltpu.make_async_remote_copy(
            src_ref=buf.at[from_slot], dst_ref=buf.at[to_slot], send_sem=send_sem,
            recv_sem=recv.at[to_slot], device_id=target, device_id_type=MESH,
        )

    for which, (buf, recv) in enumerate(((k_buf, recv_k), (v_buf, recv_v))):
        landed(buf.at[0], recv.at[0])

        @pl.when(core == 0)
        def _():
            shift(buf, 0, 2, send_shift.at[3 * which], recv, device(next_x, y, flipped, 0)).start()
            shift(buf, 0, 1, send_shift.at[3 * which + 1], recv, device(x, y, z, 1)).start()

        @pl.when(core == 1)
        def _():
            shift(buf, 0, 1, send_shift.at[3 * which], recv, device(next_x, y, flipped, 0)).start()

    for which, (buf, recv) in enumerate(((k_buf, recv_k), (v_buf, recv_v))):
        landed(buf.at[1], recv.at[1])

        @pl.when(core == 0)
        def _():
            shift(buf, 1, 2, send_shift.at[3 * which + 2], recv, device(x, y, z, 1)).start()

    limits = []
    for step in range(WIN + 1):
        earlier = jnp.maximum(span - step, 0)
        limit = lengths[earlier]
        if step > 0:
            limit = jnp.where((span - step >= 0) & (span_mask[span, step - 1] == 1), limit, 0)
        limits.append(limit)
    gain_copy.wait()
    level = levels[span]
    gain_row = jnp.sum(
        jnp.where(lax.broadcasted_iota(jnp.int32, gain_buf.shape, 0) == level, gain_buf[...], 0.0),
        axis=0, keepdims=True,
    )
    scale = LOG2E / (HD ** 0.5)

    for buf, recv in ((k_buf, recv_k), (v_buf, recv_v)):
        landed(buf.at[2], recv.at[2])

    def attend(turn, carry):
        yy = lax.rem(y + NY - turn, NY)
        base = pl.multiple_of(yy * chunk, chunk)
        landed(q_buf.at[pl.ds(base, chunk), :], recv_q.at[yy])

        def block(index, inner):
            spot = pl.ds(pl.multiple_of(base + index * QB, QB), QB)
            queries = q_buf[spot, :]
            scores = []
            for step in range(WIN + 1):
                part = lax.dot_general(
                    queries, k_buf[step], (((1,), (1,)), ((), ())), preferred_element_type=jnp.float32
                )
                live = lax.broadcasted_iota(jnp.int32, (1, slots), 1) < limits[step]
                scores.append(jnp.where(live, part, NEG))
            top = functools.reduce(
                jnp.maximum, [jnp.max(part, axis=-1, keepdims=True) for part in scores]
            )
            total = jnp.zeros((QB, 1), jnp.float32)
            mixed = jnp.zeros((QB, HD), jnp.float32)
            for step in range(WIN + 1):
                expd = jnp.exp2((scores[step] - top) * scale)
                total += jnp.sum(expd, axis=-1, keepdims=True)
                mixed += jnp.dot(
                    expd.astype(jnp.bfloat16), v_buf[step], preferred_element_type=jnp.float32
                )
            o_buf[spot, :] = (mixed / total * gain_row).astype(jnp.bfloat16)
            return inner

        lax.fori_loop(0, chunk // QB, block, 0)

        def give(zz, inner):
            block_rows = pl.ds(pl.multiple_of(base + zz * rows, rows), rows)
            done = o_buf.at[block_rows, :]
            target = out.at[:, pl.ds(pl.multiple_of(head * HD, HD), HD)]
            own = stays & (yy == y) & (zz == z_lo)

            @pl.when(own)
            def _():
                pltpu.make_async_copy(done, target, recv_o).start()

            @pl.when(jnp.logical_not(own))
            def _():
                pltpu.make_async_remote_copy(
                    src_ref=done, dst_ref=target, send_sem=send_o, recv_sem=recv_o,
                    device_id=device(x, yy, upper * NZ + zz, core), device_id_type=MESH,
                ).start()

            return inner

        lax.fori_loop(0, NZ, give, 0)
        return carry

    lax.fori_loop(0, NY, attend, 0)

    landed(out, recv_o)
    remote = (NY * NZ - 1) * HD
    for ref, sem in ((k_in, send_k), (v_in, send_v), (q_in, send_q), (q_in, send_o)):
        landed(ref.at[:, pl.ds(0, remote)], sem)

        @pl.when(jnp.logical_not(stays))
        def _():
            landed(ref.at[:, pl.ds(remote, HD)], sem)

    for which, buf in enumerate((k_buf, v_buf)):
        landed(buf.at[0], send_shift.at[3 * which])

        @pl.when(core == 0)
        def _():
            landed(buf.at[0], send_shift.at[3 * which + 1])
            landed(buf.at[1], send_shift.at[3 * which + 2])


def per_device(queries, keys, values, lengths, span_mask, levels, level_gain):
    _, rows, width = queries.shape
    slots = rows * NY * NZ
    hbm = pl.BlockSpec(memory_space=pl.ANY)
    smem = pl.BlockSpec(memory_space=pltpu.SMEM)
    dma = pltpu.SemaphoreType.DMA
    result = pl.pallas_call(
        attend_kernel,
        out_shape=jax.ShapeDtypeStruct((rows, width), jnp.bfloat16),
        in_specs=[smem, smem, smem, hbm, hbm, hbm, hbm],
        out_specs=hbm,
        scratch_shapes=[
            pltpu.VMEM((slots, HD), jnp.bfloat16),
            pltpu.VMEM((WIN + 1, slots, HD), jnp.bfloat16),
            pltpu.VMEM((WIN + 1, slots, HD), jnp.bfloat16),
            pltpu.VMEM((slots, HD), jnp.bfloat16),
            pltpu.VMEM((level_gain.shape[0], HD), jnp.float32),
            dma, dma, dma, dma, dma((6,)),
            dma((WIN + 1,)), dma((WIN + 1,)), dma((NY,)), dma, dma,
        ],
        compiler_params=pltpu.CompilerParams(
            collective_id=0, has_side_effects=True, vmem_limit_bytes=32 * 1024 * 1024
        ),
    )(lengths, span_mask, levels, queries[0], keys[0], values[0], level_gain)
    return result[None]


def solution(mesh):
    placed = (
        P("span", "seq", None),
        P("span", "seq", None),
        P("span", "seq", None),
        P(),
        P(),
        P(),
        P(),
    )
    return jax.shard_map(
        per_device, mesh=mesh, in_specs=placed, out_specs=P("span", "seq", None), check_vma=False
    )
```

```python
import functools

import jax
import jax.numpy as jnp
from jax import lax
from jax.experimental import pallas as pl
from jax.experimental.pallas import tpu as pltpu
from jax.sharding import PartitionSpec as P

HD = 128
WIN = 2
NX, NY, NZ = 4, 4, 8
CORES = 2
QB = 128
MESH = pl.DeviceIdType.MESH
NEG = -1e30
LOG2E = 1.4426950408889634


def group_x(group):
    return jnp.where(group < 4, lax.rem(group + 3, NX), lax.rem(10 - group, NX))


def attend_kernel(
    lengths, span_mask, levels, q_in, k_in, v_in, gain_in, out,
    q_buf, k_buf, v_buf, o_buf, gain_buf,
    send_k, send_v, send_q, send_o, send_shift,
    recv_k, recv_v, recv_q, recv_o, gain_sem,
):
    rows = q_in.shape[0]
    slots = k_buf.shape[1]
    span_count = lengths.shape[0]
    chunk = slots // NY
    here = lax.axis_index("span")
    member = lax.axis_index("seq")
    x, z_hi, core = here // 4, lax.rem(here // 2, 2), lax.rem(here, 2)
    y, z_lo = member // NZ, lax.rem(member, NZ)
    z = z_hi * NZ + z_lo
    home = 2 * x + z_hi
    odd = lax.rem(y + z, 2)
    group = jnp.where(odd == 0, lax.rem(x + 1, NX), NX + lax.rem(6 - x, NX))
    span = CORES * group + core
    head = (y // 2) * (2 * NZ) + z
    stays = group == home
    first, last = group == 0, group == 2 * NX - 1

    def device(xx, yy, zz, cc):
        return (xx * 4 + (zz // NZ) * 2 + cc, yy * NZ + lax.rem(zz, NZ))

    def token_place(yy, zz):
        return device(group // 2, yy, lax.rem(group, 2) * NZ + zz, core)

    def beside(other, cc):
        return device(group_x(other), 2 * (y // 2) + lax.rem(other // NX + z, 2), z, cc)

    def after(cc):
        return beside(lax.rem(group + 1, 2 * NX), cc)

    def before(cc):
        return beside(lax.rem(group + 2 * NX - 1, 2 * NX), cc)

    barrier = pltpu.get_barrier_semaphore()

    def greet(index, carry):
        yy, zz = index // NZ, lax.rem(index, NZ)

        @pl.when(jnp.logical_not(stays & (index == member)))
        def _():
            pl.semaphore_signal(
                barrier, inc=1, device_id=token_place(yy, zz), device_id_type=MESH
            )

        return carry

    lax.fori_loop(0, NY * NZ, greet, 0)

    @pl.when((core == 0) & jnp.logical_not(first))
    def _():
        for cc in range(CORES):
            pl.semaphore_signal(barrier, inc=1, device_id=before(cc), device_id_type=MESH)

    @pl.when(core == 1)
    def _():
        pl.semaphore_signal(barrier, inc=1, device_id=beside(group, 0), device_id_type=MESH)

    gain_copy = pltpu.make_async_copy(
        gain_in.at[:, pl.ds(pl.multiple_of(head * HD, HD), HD)], gain_buf, gain_sem
    )
    gain_copy.start()

    pl.semaphore_wait(
        barrier, NY * NZ + 2 - core - jnp.where(stays, 1, 0) - jnp.where(last, 1, 0)
    )

    def exchange(source, landing, send_sem, recv_sem):
        def step(index, carry):
            turn, place = index // (2 * NZ), 2 * NZ - 1 - lax.rem(index, 2 * NZ)
            half = lax.rem(y // 2 + turn, 2)
            away = ((place + 1) // 2) * (2 * lax.rem(place, 2) - 1)
            zz = lax.rem(z + away + 2 * NZ, 2 * NZ)
            yy = 2 * half + lax.rem(home // NX + zz, 2)
            columns = pl.ds(pl.multiple_of((half * 2 * NZ + zz) * HD, HD), HD)
            block = source.at[:, columns]
            target = landing.at[pl.ds(pl.multiple_of(member * rows, rows), rows), :]
            own = stays & (yy == y) & (zz == z)

            @pl.when(own)
            def _():
                pltpu.make_async_copy(block, target, recv_sem).start()

            @pl.when(jnp.logical_not(own))
            def _():
                pltpu.make_async_remote_copy(
                    src_ref=block, dst_ref=target, send_sem=send_sem, recv_sem=recv_sem,
                    device_id=device(group_x(home), yy, zz, core), device_id_type=MESH,
                ).start()

            return carry

        lax.fori_loop(0, NY * NZ, step, 0)

    exchange(k_in, k_buf.at[0], send_k, recv_k.at[0])
    exchange(v_in, v_buf.at[0], send_v, recv_v.at[0])
    exchange(q_in, q_buf, send_q, recv_q.at[y])

    def landed(ref, sem):
        pltpu.make_async_copy(ref, ref, sem).wait()

    def shift(buf, from_slot, to_slot, send_sem, recv, target):
        return pltpu.make_async_remote_copy(
            src_ref=buf.at[from_slot], dst_ref=buf.at[to_slot], send_sem=send_sem,
            recv_sem=recv.at[to_slot], device_id=target, device_id_type=MESH,
        )

    @pl.when(first)
    def _():
        @pl.when(core == 0)
        def _():
            k_buf[1] = jnp.zeros(k_buf.shape[1:], k_buf.dtype)
            v_buf[1] = jnp.zeros(v_buf.shape[1:], v_buf.dtype)

        k_buf[2] = jnp.zeros(k_buf.shape[1:], k_buf.dtype)
        v_buf[2] = jnp.zeros(v_buf.shape[1:], v_buf.dtype)

    ahead = jnp.logical_not(last)
    for which, (buf, recv) in enumerate(((k_buf, recv_k), (v_buf, recv_v))):
        landed(buf.at[0], recv.at[0])

        @pl.when(core == 0)
        def _():
            @pl.when(ahead)
            def _():
                shift(buf, 0, 2, send_shift.at[3 * which], recv, after(0)).start()

            shift(buf, 0, 1, send_shift.at[3 * which + 1], recv, beside(group, 1)).start()

        @pl.when((core == 1) & ahead)
        def _():
            shift(buf, 0, 1, send_shift.at[3 * which], recv, after(0)).start()

    behind = jnp.logical_not(first)
    for which, (buf, recv) in enumerate(((k_buf, recv_k), (v_buf, recv_v))):

        @pl.when((core == 0) & behind)
        def _():
            landed(buf.at[1], recv.at[1])
            shift(buf, 1, 2, send_shift.at[3 * which + 2], recv, beside(group, 1)).start()

        @pl.when(core == 1)
        def _():
            landed(buf.at[1], recv.at[1])

    limits = []
    for step in range(WIN + 1):
        earlier = jnp.maximum(span - step, 0)
        limit = lengths[earlier]
        if step > 0:
            limit = jnp.where((span - step >= 0) & (span_mask[span, step - 1] == 1), limit, 0)
        limits.append(limit)
    gain_copy.wait()
    level = levels[span]
    gain_row = jnp.sum(
        jnp.where(lax.broadcasted_iota(jnp.int32, gain_buf.shape, 0) == level, gain_buf[...], 0.0),
        axis=0, keepdims=True,
    )
    scale = LOG2E / (HD ** 0.5)

    @pl.when(behind)
    def _():
        for buf, recv in ((k_buf, recv_k), (v_buf, recv_v)):
            landed(buf.at[2], recv.at[2])

    near_run = jnp.where(lax.rem(group, 2) == z_hi, NZ // 2, 0)

    def attend(turn, carry):
        yy = lax.rem(y - lax.rem(y, 2) + turn, NY)
        base = pl.multiple_of(yy * chunk, chunk)
        landed(q_buf.at[pl.ds(base, chunk), :], recv_q.at[yy])

        def block(index, inner):
            spot = pl.ds(pl.multiple_of(base + index * QB, QB), QB)
            queries = q_buf[spot, :]
            scores = []
            for step in range(WIN + 1):
                part = lax.dot_general(
                    queries, k_buf[step], (((1,), (1,)), ((), ())), preferred_element_type=jnp.float32
                )
                live = lax.broadcasted_iota(jnp.int32, (1, slots), 1) < limits[step]
                scores.append(jnp.where(live, part, NEG))
            top = functools.reduce(
                jnp.maximum, [jnp.max(part, axis=-1, keepdims=True) for part in scores]
            )
            total = jnp.zeros((QB, 1), jnp.float32)
            mixed = jnp.zeros((QB, HD), jnp.float32)
            for step in range(WIN + 1):
                expd = jnp.exp2((scores[step] - top) * scale)
                total += jnp.sum(expd, axis=-1, keepdims=True)
                mixed += jnp.dot(
                    expd.astype(jnp.bfloat16), v_buf[step], preferred_element_type=jnp.float32
                )
            o_buf[spot, :] = (mixed / total * gain_row).astype(jnp.bfloat16)
            return inner

        lax.fori_loop(0, chunk // QB, block, 0)

        def give(index, inner):
            away = ((index + 1) // 2) * (2 * lax.rem(index, 2) - 1)
            zz = lax.rem(z_lo + near_run + away + NZ, NZ)
            block_rows = pl.ds(pl.multiple_of(base + zz * rows, rows), rows)
            done = o_buf.at[block_rows, :]
            target = out.at[:, pl.ds(pl.multiple_of(head * HD, HD), HD)]
            own = stays & (yy == y) & (zz == z_lo)

            @pl.when(own)
            def _():
                pltpu.make_async_copy(done, target, recv_o).start()

            @pl.when(jnp.logical_not(own))
            def _():
                pltpu.make_async_remote_copy(
                    src_ref=done, dst_ref=target, send_sem=send_o, recv_sem=recv_o,
                    device_id=token_place(yy, zz), device_id_type=MESH,
                ).start()

            return inner

        lax.fori_loop(0, NZ, give, 0)
        return carry

    lax.fori_loop(0, NY, attend, 0)

    landed(out, recv_o)
    remote = (NY * NZ - 1) * HD
    for ref, sem in ((k_in, send_k), (v_in, send_v), (q_in, send_q), (q_in, send_o)):
        landed(ref.at[:, pl.ds(0, remote)], sem)

        @pl.when(jnp.logical_not(stays))
        def _():
            landed(ref.at[:, pl.ds(remote, HD)], sem)

    for which, buf in enumerate((k_buf, v_buf)):

        @pl.when(ahead)
        def _():
            landed(buf.at[0], send_shift.at[3 * which])

        @pl.when(core == 0)
        def _():
            landed(buf.at[0], send_shift.at[3 * which + 1])

        @pl.when((core == 0) & behind)
        def _():
            landed(buf.at[1], send_shift.at[3 * which + 2])


def per_device(queries, keys, values, lengths, span_mask, levels, level_gain):
    _, rows, width = queries.shape
    slots = rows * NY * NZ
    hbm = pl.BlockSpec(memory_space=pl.ANY)
    smem = pl.BlockSpec(memory_space=pltpu.SMEM)
    dma = pltpu.SemaphoreType.DMA
    result = pl.pallas_call(
        attend_kernel,
        out_shape=jax.ShapeDtypeStruct((rows, width), jnp.bfloat16),
        in_specs=[smem, smem, smem, hbm, hbm, hbm, hbm],
        out_specs=pl.BlockSpec(memory_space=pl.ANY),
        scratch_shapes=[
            pltpu.VMEM((slots, HD), jnp.bfloat16),
            pltpu.VMEM((WIN + 1, slots, HD), jnp.bfloat16),
            pltpu.VMEM((WIN + 1, slots, HD), jnp.bfloat16),
            pltpu.VMEM((slots, HD), jnp.bfloat16),
            pltpu.VMEM((level_gain.shape[0], HD), jnp.float32),
            dma, dma, dma, dma, dma((6,)),
            dma((WIN + 1,)), dma((WIN + 1,)), dma((NY,)), dma, dma,
        ],
        compiler_params=pltpu.CompilerParams(
            collective_id=0, has_side_effects=True, vmem_limit_bytes=60 * 1024 * 1024
        ),
    )(lengths, span_mask, levels, queries[0], keys[0], values[0], level_gain)
    return result[None]


def solution(mesh):
    placed = (
        P("span", "seq", None),
        P("span", "seq", None),
        P("span", "seq", None),
        P(),
        P(),
        P(),
        P(),
    )
    return jax.shard_map(
        per_device, mesh=mesh, in_specs=placed, out_specs=P("span", "seq", None), check_vma=False
    )
```

```python
import functools

import jax
import jax.numpy as jnp
from jax import lax
from jax.experimental import pallas as pl
from jax.experimental.pallas import tpu as pltpu
from jax.sharding import PartitionSpec as P

HD = 128
WIN = 2
NX, NY, NZ = 4, 4, 8
CORES = 2
QB = 128
MESH = pl.DeviceIdType.MESH
NEG = -1e30
LOG2E = 1.4426950408889634


def group_x(group):
    return jnp.where(group < 4, lax.rem(group + 3, NX), lax.rem(10 - group, NX))


def attend_kernel(
    lengths_in, mask_in, levels_in, q_in, k_in, v_in, gain_in, out,
    lengths, span_mask, levels,
    q_buf, k_buf, v_buf, o_buf, gain_buf,
    send_k, send_v, send_q, send_o, send_shift,
    recv_k, recv_v, recv_q, recv_o, gain_sem, scalar_sem,
):
    rows = q_in.shape[0]
    slots = k_buf.shape[1]
    chunk = slots // NY
    here = lax.axis_index("span")
    member = lax.axis_index("seq")
    x, z_hi, core = here // 4, lax.rem(here // 2, 2), lax.rem(here, 2)
    y, z_lo = member // NZ, lax.rem(member, NZ)
    z = z_hi * NZ + z_lo
    home = 2 * x + z_hi
    odd = lax.rem(y + core, 2)
    group = jnp.where(odd == 0, lax.rem(x + 1, NX), NX + lax.rem(6 - x, NX))
    span = CORES * group + core
    head = (y // 2) * (2 * NZ) + z
    stays = group == home
    first, last = group == 0, group == 2 * NX - 1

    def device(xx, yy, zz, cc):
        return (xx * 4 + (zz // NZ) * 2 + cc, yy * NZ + lax.rem(zz, NZ))

    def token_place(yy, zz):
        return device(group // 2, yy, lax.rem(group, 2) * NZ + zz, core)

    def beside(other, cc):
        return device(group_x(other), 2 * (y // 2) + lax.rem(other // NX + cc, 2), z, cc)

    def after(cc):
        return beside(lax.rem(group + 1, 2 * NX), cc)

    def before(cc):
        return beside(lax.rem(group + 2 * NX - 1, 2 * NX), cc)

    scalar_copies = [
        pltpu.make_async_copy(source, held, scalar_sem.at[index])
        for index, (source, held) in enumerate(
            ((lengths_in, lengths), (mask_in, span_mask), (levels_in, levels))
        )
    ]
    for copy in scalar_copies:
        copy.start()
    barrier = pltpu.get_barrier_semaphore()

    run = lax.rem(group, 2)
    far = z_lo + jnp.where(run == z_hi, NZ // 2, 0) + NZ

    def token_slot(index):
        away = ((index + 1) // 2) * (2 * lax.rem(index, 2) - 1)
        return lax.rem(far + away, NZ)

    def greet(index, carry):
        yy, zz = lax.rem(index, NY), token_slot(index // NY)

        @pl.when(jnp.logical_not(stays & (yy == y) & (zz == z_lo)))
        def _():
            pl.semaphore_signal(
                barrier, inc=1, device_id=token_place(yy, zz), device_id_type=MESH
            )

        return carry

    lax.fori_loop(0, NY * NZ, greet, 0)

    @pl.when((core == 0) & jnp.logical_not(first))
    def _():
        for cc in range(CORES):
            pl.semaphore_signal(barrier, inc=1, device_id=before(cc), device_id_type=MESH)

    @pl.when((core == 1) & jnp.logical_not(first))
    def _():
        pl.semaphore_signal(barrier, inc=1, device_id=before(1), device_id_type=MESH)

    @pl.when(core == 1)
    def _():
        pl.semaphore_signal(barrier, inc=1, device_id=beside(group, 0), device_id_type=MESH)

    gain_copy = pltpu.make_async_copy(
        gain_in.at[:, pl.ds(pl.multiple_of(head * HD, HD), HD)], gain_buf, gain_sem
    )
    gain_copy.start()

    pl.semaphore_wait(
        barrier, NY * NZ + 2 - jnp.where(stays, 1, 0) - jnp.where(last, 1 + core, 0)
    )

    def exchange(source, landing, send_sem, recv_sem, turns=(0, 1)):
        def step(index, carry):
            turn, place = index // (2 * NZ), 2 * NZ - 1 - lax.rem(index, 2 * NZ)
            half = lax.rem(y // 2 + turn, 2)
            away = ((place + 1) // 2) * (2 * lax.rem(place, 2) - 1)
            zz = lax.rem(z + away + 2 * NZ, 2 * NZ)
            yy = 2 * half + lax.rem(home // NX + core, 2)
            columns = pl.ds(pl.multiple_of((half * 2 * NZ + zz) * HD, HD), HD)
            block = source.at[:, columns]
            target = landing.at[pl.ds(pl.multiple_of(member * rows, rows), rows), :]
            own = stays & (yy == y) & (zz == z)

            @pl.when(own)
            def _():
                pltpu.make_async_copy(block, target, recv_sem).start()

            @pl.when(jnp.logical_not(own))
            def _():
                pltpu.make_async_remote_copy(
                    src_ref=block, dst_ref=target, send_sem=send_sem, recv_sem=recv_sem,
                    device_id=device(group_x(home), yy, zz, core), device_id_type=MESH,
                ).start()

            return carry

        lax.fori_loop(2 * NZ * turns[0], 2 * NZ * (turns[-1] + 1), step, 0)

    exchange(k_in, k_buf.at[0], send_k, recv_k.at[0])
    exchange(v_in, v_buf.at[0], send_v, recv_v.at[0])
    exchange(q_in, q_buf, send_q, recv_q.at[y], (0,))

    def landed(ref, sem):
        pltpu.make_async_copy(ref, ref, sem).wait()

    def shift(buf, from_slot, to_slot, send_sem, recv, target):
        return pltpu.make_async_remote_copy(
            src_ref=buf.at[from_slot], dst_ref=buf.at[to_slot], send_sem=send_sem,
            recv_sem=recv.at[to_slot], device_id=target, device_id_type=MESH,
        )

    @pl.when(first)
    def _():
        @pl.when(core == 0)
        def _():
            k_buf[1] = jnp.zeros(k_buf.shape[1:], k_buf.dtype)
            v_buf[1] = jnp.zeros(v_buf.shape[1:], v_buf.dtype)

        k_buf[2] = jnp.zeros(k_buf.shape[1:], k_buf.dtype)
        v_buf[2] = jnp.zeros(v_buf.shape[1:], v_buf.dtype)

    ahead = jnp.logical_not(last)
    for which, (buf, recv) in enumerate(((k_buf, recv_k), (v_buf, recv_v))):
        landed(buf.at[0], recv.at[0])

        @pl.when(core == 0)
        def _():
            @pl.when(ahead)
            def _():
                shift(buf, 0, 2, send_shift.at[3 * which], recv, after(0)).start()

            shift(buf, 0, 1, send_shift.at[3 * which + 1], recv, beside(group, 1)).start()

        @pl.when((core == 1) & ahead)
        def _():
            shift(buf, 0, 1, send_shift.at[3 * which], recv, after(0)).start()
            shift(buf, 0, 2, send_shift.at[3 * which + 2], recv, after(1)).start()

    exchange(q_in, q_buf, send_q, recv_q.at[y], (1,))
    behind = jnp.logical_not(first)
    for copy in scalar_copies:
        copy.wait()
    limits = []
    for step in range(WIN + 1):
        earlier = jnp.maximum(span - step, 0)
        limit = lengths[earlier]
        if step > 0:
            limit = jnp.where((span - step >= 0) & (span_mask[step - 1, span] == 1), limit, 0)
        limits.append(limit)
    gain_copy.wait()
    level = levels[span]
    gain_row = jnp.sum(
        jnp.where(lax.broadcasted_iota(jnp.int32, gain_buf.shape, 0) == level, gain_buf[...], 0.0),
        axis=0, keepdims=True,
    )
    scale = LOG2E / (HD ** 0.5)

    for buf, recv in ((k_buf, recv_k), (v_buf, recv_v)):

        @pl.when(behind)
        def _():
            landed(buf.at[2], recv.at[2])

        @pl.when(behind | (core == 1))
        def _():
            landed(buf.at[1], recv.at[1])

    per_chunk = chunk // QB
    per_block = QB // rows

    def attend(index, carry):
        turn, part = index // per_chunk, lax.rem(index, per_chunk)
        yy = lax.rem(y - lax.rem(y, 2) + turn, NY)
        base = pl.multiple_of(yy * chunk, chunk)

        @pl.when(part == 0)
        def _():
            landed(q_buf.at[pl.ds(base, chunk), :], recv_q.at[yy])

        first_slot = lax.rem(part + far // per_block, per_chunk) * per_block
        spot = pl.ds(pl.multiple_of(base + first_slot * rows, QB), QB)
        queries = q_buf[spot, :]
        scores = []
        for step in range(WIN + 1):
            part_scores = lax.dot_general(
                queries, k_buf[step], (((1,), (1,)), ((), ())), preferred_element_type=jnp.float32
            )
            live = lax.broadcasted_iota(jnp.int32, (1, slots), 1) < limits[step]
            scores.append(jnp.where(live, part_scores, NEG))
        top = functools.reduce(
            jnp.maximum, [jnp.max(part_scores, axis=-1, keepdims=True) for part_scores in scores]
        )
        total = jnp.zeros((QB, 1), jnp.float32)
        mixed = jnp.zeros((QB, HD), jnp.float32)
        for step in range(WIN + 1):
            expd = jnp.exp2((scores[step] - top) * scale)
            total += jnp.sum(expd, axis=-1, keepdims=True)
            mixed += jnp.dot(
                expd.astype(jnp.bfloat16), v_buf[step], preferred_element_type=jnp.float32
            )
        o_buf[spot, :] = (mixed / total * gain_row).astype(jnp.bfloat16)

        def give(offset, inner):
            zz = first_slot + lax.rem(far + offset, per_block)
            block_rows = pl.ds(pl.multiple_of(base + zz * rows, rows), rows)
            done = o_buf.at[block_rows, :]
            target = out.at[:, pl.ds(pl.multiple_of(head * HD, HD), HD)]
            own = stays & (yy == y) & (zz == z_lo)

            @pl.when(own)
            def _():
                pltpu.make_async_copy(done, target, recv_o).start()

            @pl.when(jnp.logical_not(own))
            def _():
                pltpu.make_async_remote_copy(
                    src_ref=done, dst_ref=target, send_sem=send_o, recv_sem=recv_o,
                    device_id=token_place(yy, zz), device_id_type=MESH,
                ).start()

            return inner

        lax.fori_loop(0, per_block, give, 0)
        return carry

    lax.fori_loop(0, NY * per_chunk, attend, 0)

    landed(out, recv_o)
    remote = (NY * NZ - 1) * HD
    for ref, sem in ((k_in, send_k), (v_in, send_v), (q_in, send_q), (q_in, send_o)):
        landed(ref.at[:, pl.ds(0, remote)], sem)

        @pl.when(jnp.logical_not(stays))
        def _():
            landed(ref.at[:, pl.ds(remote, HD)], sem)

    for which, buf in enumerate((k_buf, v_buf)):

        @pl.when(ahead)
        def _():
            landed(buf.at[0], send_shift.at[3 * which])

        @pl.when(core == 0)
        def _():
            landed(buf.at[0], send_shift.at[3 * which + 1])

        @pl.when((core == 1) & ahead)
        def _():
            landed(buf.at[0], send_shift.at[3 * which + 2])


def per_device(queries, keys, values, lengths, span_mask, levels, level_gain):
    _, rows, width = queries.shape
    slots = rows * NY * NZ
    hbm = pl.BlockSpec(memory_space=pl.ANY)
    dma = pltpu.SemaphoreType.DMA
    result = pl.pallas_call(
        attend_kernel,
        out_shape=pltpu.VMEM((rows, width), jnp.bfloat16),
        in_specs=[hbm] * 7,
        out_specs=pl.BlockSpec(memory_space=pl.ANY),
        scratch_shapes=[
            pltpu.SMEM(lengths.shape, jnp.int32),
            pltpu.SMEM(span_mask.shape[::-1], jnp.int32),
            pltpu.SMEM(levels.shape, jnp.int32),
            pltpu.VMEM((slots, HD), jnp.bfloat16),
            pltpu.VMEM((WIN + 1, slots, HD), jnp.bfloat16),
            pltpu.VMEM((WIN + 1, slots, HD), jnp.bfloat16),
            pltpu.VMEM((slots, HD), jnp.bfloat16),
            pltpu.VMEM((level_gain.shape[0], HD), jnp.float32),
            dma, dma, dma, dma, dma((6,)),
            dma((WIN + 1,)), dma((WIN + 1,)), dma((NY,)), dma, dma, dma((3,)),
        ],
        compiler_params=pltpu.CompilerParams(
            collective_id=0, has_side_effects=True, vmem_limit_bytes=60 * 1024 * 1024
        ),
    )(lengths, span_mask.T, levels, queries[0], keys[0], values[0], level_gain)
    return result[None]


def solution(mesh):
    placed = (
        P("span", "seq", None),
        P("span", "seq", None),
        P("span", "seq", None),
        P(),
        P(),
        P(),
        P(),
    )
    return jax.shard_map(
        per_device, mesh=mesh, in_specs=placed, out_specs=P("span", "seq", None), check_vma=False
    )
```

```python
import functools

import jax
import jax.numpy as jnp
from jax import lax
from jax.experimental import pallas as pl
from jax.experimental.pallas import tpu as pltpu
from jax.sharding import PartitionSpec as P

HD = 128
WIN = 2
NX, NY, NZ = 4, 4, 8
CORES = 2
QB = 128
MESH = pl.DeviceIdType.MESH
NEG = -1e30
LOG2E = 1.4426950408889634


def group_x(group):
    return jnp.where(group < 4, lax.rem(group + 3, NX), lax.rem(10 - group, NX))


def attend_kernel(
    lengths_in, mask_in, levels_in, q_in, k_in, v_in, gain_in, out,
    lengths, span_mask, levels,
    q_buf, k_buf, v_buf, o_buf, s_buf, gain_buf,
    send_k, send_v, send_q, send_o, send_shift,
    recv_k, recv_v, recv_q, recv_o, gain_sem, scalar_sem,
):
    rows = q_in.shape[0]
    slots = k_buf.shape[1]
    chunk = slots // NY
    here = lax.axis_index("span")
    member = lax.axis_index("seq")
    x, z_hi, core = here // 4, lax.rem(here // 2, 2), lax.rem(here, 2)
    y, z_lo = member // NZ, lax.rem(member, NZ)
    z = z_hi * NZ + z_lo
    home = 2 * x + z_hi
    odd = lax.rem(y + core, 2)
    group = jnp.where(odd == 0, lax.rem(x + 1, NX), NX + lax.rem(6 - x, NX))
    span = CORES * group + core
    head = (y // 2) * (2 * NZ) + z
    stays = group == home
    first, last = group == 0, group == 2 * NX - 1

    def device(xx, yy, zz, cc):
        return (xx * 4 + (zz // NZ) * 2 + cc, yy * NZ + lax.rem(zz, NZ))

    def token_place(yy, zz):
        return device(group // 2, yy, lax.rem(group, 2) * NZ + zz, core)

    def beside(other, cc):
        return device(group_x(other), 2 * (y // 2) + lax.rem(other // NX + cc, 2), z, cc)

    def after(cc):
        return beside(lax.rem(group + 1, 2 * NX), cc)

    def before(cc):
        return beside(lax.rem(group + 2 * NX - 1, 2 * NX), cc)

    barrier = pltpu.get_barrier_semaphore()

    run = lax.rem(group, 2)
    far = z_lo + jnp.where(run == z_hi, NZ // 2, 0) + NZ

    def token_slot(index):
        away = ((index + 1) // 2) * (2 * lax.rem(index, 2) - 1)
        return lax.rem(far + away, NZ)

    token_span = (group // 2) * 4 + run * 2 + core
    for index in range(NZ):
        away = ((index + 1) // 2) * (2 * (index % 2) - 1)
        zz = jnp.bitwise_and(far + away, NZ - 1)
        for yy in range(NY):
            place = zz + yy * NZ

            @pl.when(jnp.logical_not(stays & (place == member)))
            def _():
                pl.semaphore_signal(
                    barrier, inc=1, device_id=(token_span, place), device_id_type=MESH
                )

    @pl.when((core == 0) & jnp.logical_not(first))
    def _():
        for cc in range(CORES):
            pl.semaphore_signal(barrier, inc=1, device_id=before(cc), device_id_type=MESH)

    @pl.when((core == 1) & jnp.logical_not(first))
    def _():
        pl.semaphore_signal(barrier, inc=1, device_id=before(1), device_id_type=MESH)

    @pl.when(core == 1)
    def _():
        pl.semaphore_signal(barrier, inc=1, device_id=beside(group, 0), device_id_type=MESH)

    scalar_copies = [
        pltpu.make_async_copy(source, held, scalar_sem.at[index])
        for index, (source, held) in enumerate(
            ((lengths_in, lengths), (mask_in, span_mask), (levels_in, levels))
        )
    ]
    for copy in scalar_copies:
        copy.start()
    gain_copy = pltpu.make_async_copy(
        gain_in.at[:, pl.ds(pl.multiple_of(head * HD, HD), HD)], gain_buf, gain_sem
    )
    gain_copy.start()

    pl.semaphore_wait(
        barrier, NY * NZ + 2 - jnp.where(stays, 1, 0) - jnp.where(last, 1 + core, 0)
    )

    def exchange(source, landing, send_sem, recv_sem, turns=(0, 1)):
        def step(index, carry):
            turn, place = index // (2 * NZ), 2 * NZ - 1 - lax.rem(index, 2 * NZ)
            half = lax.rem(y // 2 + turn, 2)
            away = ((place + 1) // 2) * (2 * lax.rem(place, 2) - 1)
            zz = lax.rem(z + away + 2 * NZ, 2 * NZ)
            yy = 2 * half + lax.rem(home // NX + core, 2)
            columns = pl.ds(pl.multiple_of((half * 2 * NZ + zz) * HD, HD), HD)
            block = source.at[:, columns]
            target = landing.at[pl.ds(pl.multiple_of(member * rows, rows), rows), :]
            own = stays & (yy == y) & (zz == z)

            @pl.when(own)
            def _():
                pltpu.make_async_copy(block, target, recv_sem).start()

            @pl.when(jnp.logical_not(own))
            def _():
                pltpu.make_async_remote_copy(
                    src_ref=block, dst_ref=target, send_sem=send_sem, recv_sem=recv_sem,
                    device_id=device(group_x(home), yy, zz, core), device_id_type=MESH,
                ).start()

            return carry

        lax.fori_loop(2 * NZ * turns[0], 2 * NZ * (turns[-1] + 1), step, 0)

    exchange(k_in, k_buf.at[0], send_k, recv_k.at[0])
    exchange(v_in, v_buf.at[0], send_v, recv_v.at[0])
    exchange(q_in, q_buf, send_q, recv_q.at[y], (0,))

    @pl.when(lax.rem(y, 2) == 0)
    def _():
        exchange(q_in, q_buf, send_q, recv_q.at[y], (1,))


    def landed(ref, sem):
        pltpu.make_async_copy(ref, ref, sem).wait()

    def shift(buf, from_slot, to_slot, send_sem, recv, target):
        return pltpu.make_async_remote_copy(
            src_ref=buf.at[from_slot], dst_ref=buf.at[to_slot], send_sem=send_sem,
            recv_sem=recv.at[to_slot], device_id=target, device_id_type=MESH,
        )

    @pl.when(first)
    def _():
        @pl.when(core == 0)
        def _():
            k_buf[1] = jnp.zeros(k_buf.shape[1:], k_buf.dtype)
            v_buf[1] = jnp.zeros(v_buf.shape[1:], v_buf.dtype)

        k_buf[2] = jnp.zeros(k_buf.shape[1:], k_buf.dtype)
        v_buf[2] = jnp.zeros(v_buf.shape[1:], v_buf.dtype)

    ahead = jnp.logical_not(last)
    for which, (buf, recv) in enumerate(((k_buf, recv_k), (v_buf, recv_v))):
        landed(buf.at[0], recv.at[0])

        @pl.when(core == 0)
        def _():
            shift(buf, 0, 1, send_shift.at[3 * which + 1], recv, beside(group, 1)).start()

            @pl.when(ahead)
            def _():
                shift(buf, 0, 2, send_shift.at[3 * which], recv, after(0)).start()

        @pl.when((core == 1) & ahead)
        def _():
            shift(buf, 0, 1, send_shift.at[3 * which], recv, after(0)).start()
            shift(buf, 0, 2, send_shift.at[3 * which + 2], recv, after(1)).start()

    @pl.when(lax.rem(y, 2) == 1)
    def _():
        exchange(q_in, q_buf, send_q, recv_q.at[y], (1,))

    behind = jnp.logical_not(first)
    for copy in scalar_copies:
        copy.wait()
    limits = []
    for step in range(WIN + 1):
        earlier = jnp.maximum(span - step, 0)
        limit = lengths[earlier]
        if step > 0:
            limit = jnp.where((span - step >= 0) & (span_mask[step - 1, span] == 1), limit, 0)
        limits.append(limit)
    gain_copy.wait()
    level = levels[span]
    gain_row = jnp.sum(
        jnp.where(lax.broadcasted_iota(jnp.int32, gain_buf.shape, 0) == level, gain_buf[...], 0.0),
        axis=0, keepdims=True,
    )
    scale = LOG2E / (HD ** 0.5)

    for buf, recv in ((k_buf, recv_k), (v_buf, recv_v)):

        @pl.when(behind)
        def _():
            landed(buf.at[2], recv.at[2])

        @pl.when(behind | (core == 1))
        def _():
            landed(buf.at[1], recv.at[1])

    per_block = QB // rows

    def attend(turn, carry):
        yy = lax.rem(y - lax.rem(y, 2) + turn, NY)
        base = pl.multiple_of(yy * chunk, chunk)
        landed(q_buf.at[pl.ds(base, chunk), :], recv_q.at[yy])
        slot = lax.rem(far // per_block, 2) * per_block
        blocks = (slot, per_block - slot)

        def spot_of(first_slot):
            return pl.ds(pl.multiple_of(base + first_slot * rows, QB), QB)

        def score(first_slot, step):
            part = lax.dot_general(
                q_buf[spot_of(first_slot), :], k_buf[step], (((1,), (1,)), ((), ())),
                preferred_element_type=jnp.float32,
            )
            live = lax.broadcasted_iota(jnp.int32, (1, slots), 1) < limits[step]
            return jnp.where(live, part, NEG)

        def finish(first_slot, scores):
            top = functools.reduce(
                jnp.maximum, [jnp.max(part, axis=-1, keepdims=True) for part in scores]
            )
            total = jnp.zeros((QB, 1), jnp.float32)
            mixed = jnp.zeros((QB, HD), jnp.float32)
            for step in range(WIN + 1):
                expd = jnp.exp2((scores[step] - top) * scale)
                total += jnp.sum(expd, axis=-1, keepdims=True)
                mixed += jnp.dot(
                    expd.astype(jnp.bfloat16), v_buf[step], preferred_element_type=jnp.float32
                )
            o_buf[spot_of(first_slot), :] = (mixed / total * gain_row).astype(jnp.bfloat16)

        def give(offset, first_slot):
            zz = first_slot + lax.rem(far + offset, per_block)
            block_rows = pl.ds(pl.multiple_of(base + zz * rows, rows), rows)
            done = o_buf.at[block_rows, :]
            target = out.at[:, pl.ds(pl.multiple_of(head * HD, HD), HD)]
            own = stays & (yy == y) & (zz == z_lo)

            @pl.when(own)
            def _():
                pltpu.make_async_copy(done, target, recv_o).start()

            @pl.when(jnp.logical_not(own))
            def _():
                pltpu.make_async_remote_copy(
                    src_ref=done, dst_ref=target, send_sem=send_o, recv_sem=recv_o,
                    device_id=token_place(yy, zz), device_id_type=MESH,
                ).start()

            return first_slot

        scores = [score(blocks[0], step) for step in range(WIN + 1)]
        for step in range(WIN + 1):
            s_buf[step] = score(blocks[1], step)
        finish(blocks[0], scores)
        lax.fori_loop(0, per_block, give, blocks[0])
        finish(blocks[1], [s_buf[step] for step in range(WIN + 1)])
        lax.fori_loop(0, per_block, give, blocks[1])
        return carry

    lax.fori_loop(0, NY, attend, 0)

    landed(out, recv_o)
    remote = (NY * NZ - 1) * HD
    for ref, sem in ((k_in, send_k), (v_in, send_v), (q_in, send_q), (q_in, send_o)):
        landed(ref.at[:, pl.ds(0, remote)], sem)

        @pl.when(jnp.logical_not(stays))
        def _():
            landed(ref.at[:, pl.ds(remote, HD)], sem)

    for which, buf in enumerate((k_buf, v_buf)):

        @pl.when(ahead)
        def _():
            landed(buf.at[0], send_shift.at[3 * which])

        @pl.when(core == 0)
        def _():
            landed(buf.at[0], send_shift.at[3 * which + 1])

        @pl.when((core == 1) & ahead)
        def _():
            landed(buf.at[0], send_shift.at[3 * which + 2])


def per_device(queries, keys, values, lengths, span_mask, levels, level_gain):
    _, rows, width = queries.shape
    slots = rows * NY * NZ
    hbm = pl.BlockSpec(memory_space=pl.ANY)
    dma = pltpu.SemaphoreType.DMA
    result = pl.pallas_call(
        attend_kernel,
        out_shape=pltpu.VMEM((rows, width), jnp.bfloat16),
        in_specs=[hbm] * 7,
        out_specs=pl.BlockSpec(memory_space=pl.ANY),
        scratch_shapes=[
            pltpu.SMEM(lengths.shape, jnp.int32),
            pltpu.SMEM(span_mask.shape[::-1], jnp.int32),
            pltpu.SMEM(levels.shape, jnp.int32),
            pltpu.VMEM((slots, HD), jnp.bfloat16),
            pltpu.VMEM((WIN + 1, slots, HD), jnp.bfloat16),
            pltpu.VMEM((WIN + 1, slots, HD), jnp.bfloat16),
            pltpu.VMEM((slots, HD), jnp.bfloat16),
            pltpu.VMEM((WIN + 1, QB, slots), jnp.float32),
            pltpu.VMEM((level_gain.shape[0], HD), jnp.float32),
            dma, dma, dma, dma, dma((6,)),
            dma((WIN + 1,)), dma((WIN + 1,)), dma((NY,)), dma, dma, dma((3,)),
        ],
        compiler_params=pltpu.CompilerParams(
            collective_id=0, has_side_effects=True, vmem_limit_bytes=60 * 1024 * 1024
        ),
    )(lengths, span_mask.T, levels, queries[0], keys[0], values[0], level_gain)
    return result[None]


def solution(mesh):
    placed = (
        P("span", "seq", None),
        P("span", "seq", None),
        P("span", "seq", None),
        P(),
        P(),
        P(),
        P(),
    )
    return jax.shard_map(
        per_device, mesh=mesh, in_specs=placed, out_specs=P("span", "seq", None), check_vma=False
    )
```

```python
import functools

import jax
import jax.numpy as jnp
from jax import lax
from jax.experimental import pallas as pl
from jax.experimental.pallas import tpu as pltpu
from jax.sharding import PartitionSpec as P

HD = 128
WIN = 2
NX, NY, NZ = 4, 4, 8
CORES = 2
QB = 128
MESH = pl.DeviceIdType.MESH
NEG = -1e30
LOG2E = 1.4426950408889634


def group_x(group):
    return jnp.where(group < 4, lax.rem(group + 3, NX), lax.rem(10 - group, NX))


def attend_kernel(
    lengths_in, mask_in, levels_in, q_in, k_in, v_in, gain_in, out,
    lengths, span_mask, levels,
    q_buf, k_buf, v_buf, o_buf, s_buf, gain_buf,
    send_k, send_v, send_q, send_o, send_shift,
    recv_k, recv_v, recv_q, recv_o, gain_sem, scalar_sem,
):
    rows = q_in.shape[0]
    slots = k_buf.shape[1]
    chunk = slots // NY
    here = lax.axis_index("span")
    member = lax.axis_index("seq")
    x, z_hi, core = here // 4, lax.rem(here // 2, 2), lax.rem(here, 2)
    y, z_lo = member // NZ, lax.rem(member, NZ)
    z = z_hi * NZ + z_lo
    home = 2 * x + z_hi
    odd = lax.rem(y + core, 2)
    group = jnp.where(odd == 0, lax.rem(x + 1, NX), NX + lax.rem(6 - x, NX))
    span = CORES * group + core
    head = (y // 2) * (2 * NZ) + z
    stays = group == home
    first, last = group == 0, group == 2 * NX - 1

    def device(xx, yy, zz, cc):
        return (xx * 4 + (zz // NZ) * 2 + cc, yy * NZ + lax.rem(zz, NZ))

    def token_place(yy, zz):
        return device(group // 2, yy, lax.rem(group, 2) * NZ + zz, core)

    def beside(other, cc):
        return device(group_x(other), 2 * (y // 2) + lax.rem(other // NX + cc, 2), z, cc)

    def after(cc):
        return beside(lax.rem(group + 1, 2 * NX), cc)

    def before(cc):
        return beside(lax.rem(group + 2 * NX - 1, 2 * NX), cc)

    barrier = pltpu.get_barrier_semaphore()

    run = lax.rem(group, 2)
    far = z_lo + jnp.where(run == z_hi, NZ // 2, 0) + NZ

    def token_slot(index):
        away = ((index + 1) // 2) * (2 * lax.rem(index, 2) - 1)
        return lax.rem(far + away, NZ)

    token_span = (group // 2) * 4 + run * 2 + core
    for index in range(NZ):
        away = ((index + 1) // 2) * (2 * (index % 2) - 1)
        zz = jnp.bitwise_and(far + away, NZ - 1)
        for yy in range(NY):
            place = zz + yy * NZ

            @pl.when(jnp.logical_not(stays & (place == member)))
            def _():
                pl.semaphore_signal(
                    barrier, inc=1, device_id=(token_span, place), device_id_type=MESH
                )

    @pl.when((core == 0) & jnp.logical_not(first))
    def _():
        for cc in range(CORES):
            pl.semaphore_signal(barrier, inc=1, device_id=before(cc), device_id_type=MESH)

    @pl.when((core == 1) & jnp.logical_not(first))
    def _():
        pl.semaphore_signal(barrier, inc=1, device_id=before(1), device_id_type=MESH)

    @pl.when(core == 1)
    def _():
        pl.semaphore_signal(barrier, inc=1, device_id=beside(group, 0), device_id_type=MESH)

    scalar_copies = [
        pltpu.make_async_copy(source, held, scalar_sem.at[index])
        for index, (source, held) in enumerate(
            ((lengths_in, lengths), (mask_in, span_mask), (levels_in, levels))
        )
    ]
    for copy in scalar_copies:
        copy.start()
    gain_copy = pltpu.make_async_copy(
        gain_in.at[:, pl.ds(pl.multiple_of(head * HD, HD), HD)], gain_buf, gain_sem
    )
    gain_copy.start()

    pl.semaphore_wait(
        barrier, NY * NZ + 2 - jnp.where(stays, 1, 0) - jnp.where(last, 1 + core, 0)
    )

    def exchange(source, landing, send_sem, recv_sem, turns=(0, 1), swap=False):
        def step(index, carry):
            turn, place = index // (2 * NZ), 2 * NZ - 1 - lax.rem(index, 2 * NZ)
            half = lax.rem(y // 2 + turn + (1 if swap else 0), 2)
            away = ((place + 1) // 2) * (2 * lax.rem(place, 2) - 1)
            zz = lax.rem(z + away + 2 * NZ, 2 * NZ)
            yy = 2 * half + lax.rem(home // NX + core, 2)
            columns = pl.ds(pl.multiple_of((half * 2 * NZ + zz) * HD, HD), HD)
            block = source.at[:, columns]
            target = landing.at[pl.ds(pl.multiple_of(member * rows, rows), rows), :]
            own = stays & (yy == y) & (zz == z)

            @pl.when(own)
            def _():
                pltpu.make_async_copy(block, target, recv_sem).start()

            @pl.when(jnp.logical_not(own))
            def _():
                pltpu.make_async_remote_copy(
                    src_ref=block, dst_ref=target, send_sem=send_sem, recv_sem=recv_sem,
                    device_id=device(group_x(home), yy, zz, core), device_id_type=MESH,
                ).start()

            return carry

        lax.fori_loop(2 * NZ * turns[0], 2 * NZ * (turns[-1] + 1), step, 0)

    exchange(k_in, k_buf.at[0], send_k, recv_k.at[0], swap=True)
    exchange(v_in, v_buf.at[0], send_v, recv_v.at[0], swap=True)
    exchange(q_in, q_buf, send_q, recv_q.at[y], (0,))

    @pl.when(lax.rem(y, 2) == 0)
    def _():
        exchange(q_in, q_buf, send_q, recv_q.at[y], (1,))


    def landed(ref, sem):
        pltpu.make_async_copy(ref, ref, sem).wait()

    def shift(buf, from_slot, to_slot, send_sem, recv, target):
        return pltpu.make_async_remote_copy(
            src_ref=buf.at[from_slot], dst_ref=buf.at[to_slot], send_sem=send_sem,
            recv_sem=recv.at[to_slot], device_id=target, device_id_type=MESH,
        )

    @pl.when(first)
    def _():
        @pl.when(core == 0)
        def _():
            k_buf[1] = jnp.zeros(k_buf.shape[1:], k_buf.dtype)
            v_buf[1] = jnp.zeros(v_buf.shape[1:], v_buf.dtype)

        k_buf[2] = jnp.zeros(k_buf.shape[1:], k_buf.dtype)
        v_buf[2] = jnp.zeros(v_buf.shape[1:], v_buf.dtype)

    ahead = jnp.logical_not(last)
    for which, (buf, recv) in enumerate(((k_buf, recv_k), (v_buf, recv_v))):
        landed(buf.at[0], recv.at[0])

        @pl.when(core == 0)
        def _():
            shift(buf, 0, 1, send_shift.at[3 * which + 1], recv, beside(group, 1)).start()

            @pl.when(ahead)
            def _():
                shift(buf, 0, 2, send_shift.at[3 * which], recv, after(0)).start()

        @pl.when((core == 1) & ahead)
        def _():
            shift(buf, 0, 1, send_shift.at[3 * which], recv, after(0)).start()
            shift(buf, 0, 2, send_shift.at[3 * which + 2], recv, after(1)).start()

    @pl.when(lax.rem(y, 2) == 1)
    def _():
        exchange(q_in, q_buf, send_q, recv_q.at[y], (1,))

    behind = jnp.logical_not(first)
    for copy in scalar_copies:
        copy.wait()
    limits = []
    for step in range(WIN + 1):
        earlier = jnp.maximum(span - step, 0)
        limit = lengths[earlier]
        if step > 0:
            limit = jnp.where((span - step >= 0) & (span_mask[step - 1, span] == 1), limit, 0)
        limits.append(limit)
    gain_copy.wait()
    level = levels[span]
    gain_row = jnp.sum(
        jnp.where(lax.broadcasted_iota(jnp.int32, gain_buf.shape, 0) == level, gain_buf[...], 0.0),
        axis=0, keepdims=True,
    )
    scale = LOG2E / (HD ** 0.5)

    for buf, recv in ((k_buf, recv_k), (v_buf, recv_v)):

        @pl.when(behind)
        def _():
            landed(buf.at[2], recv.at[2])

        @pl.when(behind | (core == 1))
        def _():
            landed(buf.at[1], recv.at[1])

    per_block = QB // rows

    def attend(turn, carry):
        yy = lax.rem(y - lax.rem(y, 2) + turn, NY)
        base = pl.multiple_of(yy * chunk, chunk)
        landed(q_buf.at[pl.ds(base, chunk), :], recv_q.at[yy])
        slot = lax.rem(far // per_block, 2) * per_block
        blocks = (slot, per_block - slot)

        def spot_of(first_slot):
            return pl.ds(pl.multiple_of(base + first_slot * rows, QB), QB)

        def score(first_slot, step):
            part = lax.dot_general(
                q_buf[spot_of(first_slot), :], k_buf[step], (((1,), (1,)), ((), ())),
                preferred_element_type=jnp.float32,
            )
            live = lax.broadcasted_iota(jnp.int32, (1, slots), 1) < limits[step]
            return jnp.where(live, part, NEG)

        def finish(first_slot, scores):
            top = functools.reduce(
                jnp.maximum, [jnp.max(part, axis=-1, keepdims=True) for part in scores]
            )
            total = jnp.zeros((QB, 1), jnp.float32)
            mixed = jnp.zeros((QB, HD), jnp.float32)
            for step in range(WIN + 1):
                expd = jnp.exp2((scores[step] - top) * scale)
                total += jnp.sum(expd, axis=-1, keepdims=True)
                mixed += jnp.dot(
                    expd.astype(jnp.bfloat16), v_buf[step], preferred_element_type=jnp.float32
                )
            o_buf[spot_of(first_slot), :] = (mixed / total * gain_row).astype(jnp.bfloat16)

        def give(offset, first_slot):
            zz = first_slot + lax.rem(far + offset, per_block)
            block_rows = pl.ds(pl.multiple_of(base + zz * rows, rows), rows)
            done = o_buf.at[block_rows, :]
            target = out.at[:, pl.ds(pl.multiple_of(head * HD, HD), HD)]
            own = stays & (yy == y) & (zz == z_lo)

            @pl.when(own)
            def _():
                pltpu.make_async_copy(done, target, recv_o).start()

            @pl.when(jnp.logical_not(own))
            def _():
                pltpu.make_async_remote_copy(
                    src_ref=done, dst_ref=target, send_sem=send_o, recv_sem=recv_o,
                    device_id=token_place(yy, zz), device_id_type=MESH,
                ).start()

            return first_slot

        scores = [score(blocks[0], step) for step in range(WIN + 1)]
        for step in range(WIN + 1):
            s_buf[step] = score(blocks[1], step)
        finish(blocks[0], scores)
        lax.fori_loop(0, per_block, give, blocks[0])
        finish(blocks[1], [s_buf[step] for step in range(WIN + 1)])
        lax.fori_loop(0, per_block, give, blocks[1])
        return carry

    lax.fori_loop(0, NY, attend, 0)

    landed(out, recv_o)
    remote = (NY * NZ - 1) * HD
    for ref, sem in ((k_in, send_k), (v_in, send_v), (q_in, send_q), (q_in, send_o)):
        landed(ref.at[:, pl.ds(0, remote)], sem)

        @pl.when(jnp.logical_not(stays))
        def _():
            landed(ref.at[:, pl.ds(remote, HD)], sem)

    for which, buf in enumerate((k_buf, v_buf)):

        @pl.when(ahead)
        def _():
            landed(buf.at[0], send_shift.at[3 * which])

        @pl.when(core == 0)
        def _():
            landed(buf.at[0], send_shift.at[3 * which + 1])

        @pl.when((core == 1) & ahead)
        def _():
            landed(buf.at[0], send_shift.at[3 * which + 2])


def per_device(queries, keys, values, lengths, span_mask, levels, level_gain):
    _, rows, width = queries.shape
    slots = rows * NY * NZ
    hbm = pl.BlockSpec(memory_space=pl.ANY)
    dma = pltpu.SemaphoreType.DMA
    result = pl.pallas_call(
        attend_kernel,
        out_shape=pltpu.VMEM((rows, width), jnp.bfloat16),
        in_specs=[hbm] * 7,
        out_specs=pl.BlockSpec(memory_space=pl.ANY),
        scratch_shapes=[
            pltpu.SMEM(lengths.shape, jnp.int32),
            pltpu.SMEM(span_mask.shape[::-1], jnp.int32),
            pltpu.SMEM(levels.shape, jnp.int32),
            pltpu.VMEM((slots, HD), jnp.bfloat16),
            pltpu.VMEM((WIN + 1, slots, HD), jnp.bfloat16),
            pltpu.VMEM((WIN + 1, slots, HD), jnp.bfloat16),
            pltpu.VMEM((slots, HD), jnp.bfloat16),
            pltpu.VMEM((WIN + 1, QB, slots), jnp.float32),
            pltpu.VMEM((level_gain.shape[0], HD), jnp.float32),
            dma, dma, dma, dma, dma((6,)),
            dma((WIN + 1,)), dma((WIN + 1,)), dma((NY,)), dma, dma, dma((3,)),
        ],
        compiler_params=pltpu.CompilerParams(
            collective_id=0, has_side_effects=True, vmem_limit_bytes=60 * 1024 * 1024
        ),
    )(lengths, span_mask.T, levels, queries[0], keys[0], values[0], level_gain)
    return result[None]


def solution(mesh):
    placed = (
        P("span", "seq", None),
        P("span", "seq", None),
        P("span", "seq", None),
        P(),
        P(),
        P(),
        P(),
    )
    return jax.shard_map(
        per_device, mesh=mesh, in_specs=placed, out_specs=P("span", "seq", None), check_vma=False
    )
```

```python
import functools

import jax
import jax.numpy as jnp
from jax import lax
from jax.experimental import pallas as pl
from jax.experimental.pallas import tpu as pltpu
from jax.sharding import PartitionSpec as P

HD = 128
WIN = 2
NX, NY, NZ = 4, 4, 8
CORES = 2
QB = 128
MESH = pl.DeviceIdType.MESH
NEG = -3e38
LOG2E = 1.4426950408889634


def group_x(group):
    return jnp.where(group < 4, lax.rem(group + 3, NX), lax.rem(10 - group, NX))


def attend_kernel(
    lengths_in, mask_in, levels_in, q_in, k_in, v_in, gain_in, out,
    lengths, span_mask, levels,
    q_buf, k_buf, v_buf, o_buf, s_buf, gain_buf,
    send_k, send_v, send_q, send_o, send_shift,
    recv_k, recv_v, recv_q, recv_o, gain_sem, scalar_sem,
):
    rows = q_in.shape[0]
    slots = k_buf.shape[1]
    chunk = slots // NY
    here = lax.axis_index("span")
    member = lax.axis_index("seq")
    x, z_hi, core = here // 4, lax.rem(here // 2, 2), lax.rem(here, 2)
    y, z_lo = member // NZ, lax.rem(member, NZ)
    z = z_hi * NZ + z_lo
    home = 2 * x + z_hi
    odd = lax.rem(y + core, 2)
    group = jnp.where(odd == 0, lax.rem(x + 1, NX), NX + lax.rem(6 - x, NX))
    span = CORES * group + core
    head = (y // 2) * (2 * NZ) + z
    stays = group == home
    first, last = group == 0, group == 2 * NX - 1

    def device(xx, yy, zz, cc):
        return (xx * 4 + (zz // NZ) * 2 + cc, yy * NZ + lax.rem(zz, NZ))

    def token_place(yy, zz):
        return device(group // 2, yy, lax.rem(group, 2) * NZ + zz, core)

    def beside(other, cc):
        return device(group_x(other), 2 * (y // 2) + lax.rem(other // NX + cc, 2), z, cc)

    def after(cc):
        return beside(lax.rem(group + 1, 2 * NX), cc)

    def before(cc):
        return beside(lax.rem(group + 2 * NX - 1, 2 * NX), cc)

    barrier = pltpu.get_barrier_semaphore()

    run = lax.rem(group, 2)
    far = z_lo + jnp.where(run == z_hi, NZ // 2, 0) + NZ

    def token_slot(index):
        away = ((index + 1) // 2) * (2 * lax.rem(index, 2) - 1)
        return lax.rem(far + away, NZ)

    token_span = (group // 2) * 4 + run * 2 + core
    for index in range(NZ):
        away = ((index + 1) // 2) * (2 * (index % 2) - 1)
        zz = jnp.bitwise_and(far + away, NZ - 1)
        for yy in range(NY):
            place = zz + yy * NZ

            @pl.when(jnp.logical_not(stays & (place == member)))
            def _():
                pl.semaphore_signal(
                    barrier, inc=1, device_id=(token_span, place), device_id_type=MESH
                )

    @pl.when((core == 0) & jnp.logical_not(first))
    def _():
        for cc in range(CORES):
            pl.semaphore_signal(barrier, inc=1, device_id=before(cc), device_id_type=MESH)

    @pl.when((core == 1) & jnp.logical_not(first))
    def _():
        pl.semaphore_signal(barrier, inc=1, device_id=before(1), device_id_type=MESH)

    @pl.when(core == 1)
    def _():
        pl.semaphore_signal(barrier, inc=1, device_id=beside(group, 0), device_id_type=MESH)

    scalar_copies = [
        pltpu.make_async_copy(source, held, scalar_sem.at[index])
        for index, (source, held) in enumerate(
            ((lengths_in, lengths), (mask_in, span_mask), (levels_in, levels))
        )
    ]
    for copy in scalar_copies:
        copy.start()
    gain_copy = pltpu.make_async_copy(
        gain_in.at[:, pl.ds(pl.multiple_of(head * HD, HD), HD)], gain_buf, gain_sem
    )
    gain_copy.start()

    pl.semaphore_wait(
        barrier, NY * NZ + 2 - jnp.where(stays, 1, 0) - jnp.where(last, 1 + core, 0)
    )

    def exchange(source, landing, send_sem, recv_sem, turns=(0, 1), swap=False):
        def step(index, carry):
            turn, place = index // (2 * NZ), 2 * NZ - 1 - lax.rem(index, 2 * NZ)
            half = lax.rem(y // 2 + turn + (1 if swap else 0), 2)
            away = ((place + 1) // 2) * (2 * lax.rem(place, 2) - 1)
            zz = lax.rem(z + away + 2 * NZ, 2 * NZ)
            yy = 2 * half + lax.rem(home // NX + core, 2)
            columns = pl.ds(pl.multiple_of((half * 2 * NZ + zz) * HD, HD), HD)
            block = source.at[:, columns]
            target = landing.at[pl.ds(pl.multiple_of(member * rows, rows), rows), :]
            own = stays & (yy == y) & (zz == z)

            @pl.when(own)
            def _():
                pltpu.make_async_copy(block, target, recv_sem).start()

            @pl.when(jnp.logical_not(own))
            def _():
                pltpu.make_async_remote_copy(
                    src_ref=block, dst_ref=target, send_sem=send_sem, recv_sem=recv_sem,
                    device_id=device(group_x(home), yy, zz, core), device_id_type=MESH,
                ).start()

            return carry

        lax.fori_loop(2 * NZ * turns[0], 2 * NZ * (turns[-1] + 1), step, 0)

    exchange(k_in, k_buf.at[0], send_k, recv_k.at[0], swap=True)
    exchange(v_in, v_buf.at[0], send_v, recv_v.at[0], swap=True)
    exchange(q_in, q_buf, send_q, recv_q.at[y], (0,))

    @pl.when(lax.rem(y, 2) == 0)
    def _():
        exchange(q_in, q_buf, send_q, recv_q.at[y], (1,))


    def landed(ref, sem):
        pltpu.make_async_copy(ref, ref, sem).wait()

    def shift(buf, from_slot, to_slot, send_sem, recv, target):
        return pltpu.make_async_remote_copy(
            src_ref=buf.at[from_slot], dst_ref=buf.at[to_slot], send_sem=send_sem,
            recv_sem=recv.at[to_slot], device_id=target, device_id_type=MESH,
        )

    @pl.when(first)
    def _():
        @pl.when(core == 0)
        def _():
            k_buf[1] = jnp.zeros(k_buf.shape[1:], k_buf.dtype)
            v_buf[1] = jnp.zeros(v_buf.shape[1:], v_buf.dtype)

        k_buf[2] = jnp.zeros(k_buf.shape[1:], k_buf.dtype)
        v_buf[2] = jnp.zeros(v_buf.shape[1:], v_buf.dtype)

    ahead = jnp.logical_not(last)
    for which, (buf, recv) in enumerate(((k_buf, recv_k), (v_buf, recv_v))):
        landed(buf.at[0], recv.at[0])

        @pl.when(core == 0)
        def _():
            shift(buf, 0, 1, send_shift.at[3 * which + 1], recv, beside(group, 1)).start()

            @pl.when(ahead)
            def _():
                shift(buf, 0, 2, send_shift.at[3 * which], recv, after(0)).start()

        @pl.when((core == 1) & ahead)
        def _():
            shift(buf, 0, 1, send_shift.at[3 * which], recv, after(0)).start()
            shift(buf, 0, 2, send_shift.at[3 * which + 2], recv, after(1)).start()

    @pl.when(lax.rem(y, 2) == 1)
    def _():
        exchange(q_in, q_buf, send_q, recv_q.at[y], (1,))

    behind = jnp.logical_not(first)
    for copy in scalar_copies:
        copy.wait()
    limits = []
    for step in range(WIN + 1):
        earlier = jnp.maximum(span - step, 0)
        limit = lengths[earlier]
        if step > 0:
            limit = jnp.where((span - step >= 0) & (span_mask[step - 1, span] == 1), limit, 0)
        limits.append(limit)
    gain_copy.wait()
    level = levels[span]
    gain_row = jnp.sum(
        jnp.where(lax.broadcasted_iota(jnp.int32, gain_buf.shape, 0) == level, gain_buf[...], 0.0),
        axis=0, keepdims=True,
    )
    scale = LOG2E / (HD ** 0.5)

    for buf, recv in ((k_buf, recv_k), (v_buf, recv_v)):

        @pl.when(behind)
        def _():
            landed(buf.at[2], recv.at[2])

        @pl.when(behind | (core == 1))
        def _():
            landed(buf.at[1], recv.at[1])

    per_block = QB // rows

    def attend(turn, carry):
        yy = lax.rem(y - lax.rem(y, 2) + turn, NY)
        base = pl.multiple_of(yy * chunk, chunk)
        landed(q_buf.at[pl.ds(base, chunk), :], recv_q.at[yy])
        slot = lax.rem(far // per_block, 2) * per_block
        blocks = (slot, per_block - slot)

        def spot_of(first_slot):
            return pl.ds(pl.multiple_of(base + first_slot * rows, QB), QB)

        def score(first_slot, step):
            part = lax.dot_general(
                q_buf[spot_of(first_slot), :], k_buf[step], (((1,), (1,)), ((), ())),
                preferred_element_type=jnp.float32,
            )
            live = lax.broadcasted_iota(jnp.int32, (1, slots), 1) < limits[step]
            return jnp.where(live, part, NEG)

        def finish(first_slot, scores):
            top = functools.reduce(
                jnp.maximum, [jnp.max(part, axis=-1, keepdims=True) for part in scores]
            )
            total = jnp.zeros((QB, 1), jnp.float32)
            mixed = jnp.zeros((QB, HD), jnp.float32)
            for step in range(WIN + 1):
                expd = jnp.exp2((scores[step] - top) * scale)
                total += jnp.sum(expd, axis=-1, keepdims=True)
                mixed += jnp.dot(
                    expd.astype(jnp.bfloat16), v_buf[step], preferred_element_type=jnp.float32
                )
            o_buf[spot_of(first_slot), :] = (mixed / total * gain_row).astype(jnp.bfloat16)

        def give(offset, first_slot):
            zz = first_slot + lax.rem(far + offset, per_block)
            block_rows = pl.ds(pl.multiple_of(base + zz * rows, rows), rows)
            done = o_buf.at[block_rows, :]
            target = out.at[:, pl.ds(pl.multiple_of(head * HD, HD), HD)]
            own = stays & (yy == y) & (zz == z_lo)

            @pl.when(own)
            def _():
                pltpu.make_async_copy(done, target, recv_o).start()

            @pl.when(jnp.logical_not(own))
            def _():
                pltpu.make_async_remote_copy(
                    src_ref=done, dst_ref=target, send_sem=send_o, recv_sem=recv_o,
                    device_id=token_place(yy, zz), device_id_type=MESH,
                ).start()

            return first_slot

        scores = [score(blocks[0], step) for step in range(WIN + 1)]
        for step in range(WIN + 1):
            s_buf[step] = score(blocks[1], step)
        finish(blocks[0], scores)
        lax.fori_loop(0, per_block, give, blocks[0])
        finish(blocks[1], [s_buf[step] for step in range(WIN + 1)])
        lax.fori_loop(0, per_block, give, blocks[1])
        return carry

    lax.fori_loop(0, NY, attend, 0)

    landed(out, recv_o)
    remote = (NY * NZ - 1) * HD
    for ref, sem in ((k_in, send_k), (v_in, send_v), (q_in, send_q), (q_in, send_o)):
        landed(ref.at[:, pl.ds(0, remote)], sem)

        @pl.when(jnp.logical_not(stays))
        def _():
            landed(ref.at[:, pl.ds(remote, HD)], sem)

    for which, buf in enumerate((k_buf, v_buf)):

        @pl.when(ahead)
        def _():
            landed(buf.at[0], send_shift.at[3 * which])

        @pl.when(core == 0)
        def _():
            landed(buf.at[0], send_shift.at[3 * which + 1])

        @pl.when((core == 1) & ahead)
        def _():
            landed(buf.at[0], send_shift.at[3 * which + 2])


def per_device(queries, keys, values, lengths, span_mask, levels, level_gain):
    _, rows, width = queries.shape
    slots = rows * NY * NZ
    hbm = pl.BlockSpec(memory_space=pl.ANY)
    dma = pltpu.SemaphoreType.DMA
    result = pl.pallas_call(
        attend_kernel,
        out_shape=pltpu.VMEM((rows, width), jnp.bfloat16),
        in_specs=[hbm] * 7,
        out_specs=pl.BlockSpec(memory_space=pl.ANY),
        scratch_shapes=[
            pltpu.SMEM(lengths.shape, jnp.int32),
            pltpu.SMEM(span_mask.shape[::-1], jnp.int32),
            pltpu.SMEM(levels.shape, jnp.int32),
            pltpu.VMEM((slots, HD), jnp.bfloat16),
            pltpu.VMEM((WIN + 1, slots, HD), jnp.bfloat16),
            pltpu.VMEM((WIN + 1, slots, HD), jnp.bfloat16),
            pltpu.VMEM((slots, HD), jnp.bfloat16),
            pltpu.VMEM((WIN + 1, QB, slots), jnp.float32),
            pltpu.VMEM((level_gain.shape[0], HD), jnp.float32),
            dma, dma, dma, dma, dma((6,)),
            dma((WIN + 1,)), dma((WIN + 1,)), dma((NY,)), dma, dma, dma((3,)),
        ],
        compiler_params=pltpu.CompilerParams(
            collective_id=0, has_side_effects=True, vmem_limit_bytes=60 * 1024 * 1024
        ),
    )(lengths, span_mask.T, levels, queries[0], keys[0], values[0], level_gain)
    return result[None]


def solution(mesh):
    placed = (
        P("span", "seq", None),
        P("span", "seq", None),
        P("span", "seq", None),
        P(),
        P(),
        P(),
        P(),
    )
    return jax.shard_map(
        per_device, mesh=mesh, in_specs=placed, out_specs=P("span", "seq", None), check_vma=False
    )
```
